256 devices in a mesh: frames: 16 (over z_lo, y, core), heads: 16 (over x, z_hi).
Axes of the slice: x: 4, y: 4, z: 8 (z_hi: 4, z_lo: 2; z = z_hi * 2 + z_lo), core: 2. Of those that a mesh axis runs over, the one named last changes fastest.
Arguments:
- query_spatial: bfloat16 [32, 1024, 2048], P('frames', None, 'heads'), may hold values from -6 to 6
- key_spatial: bfloat16 [32, 1024, 2048], P('frames', None, 'heads'), may hold values from -6 to 6
- value_spatial: bfloat16 [32, 1024, 2048], P('frames', None, 'heads'), may hold values from -6 to 6
- output_spatial: bfloat16 [32, 1024, 2048], P('frames', None, 'heads'), may hold values from -6 to 6
- grad_spatial: bfloat16 [32, 1024, 2048], P('frames', None, 'heads'), may hold values from -96 to 96
- query_temporal: bfloat16 [2, 16, 1024, 2048], P(None, 'frames', None, 'heads'), may hold values from -6 to 6
- key_temporal: bfloat16 [2, 16, 1024, 2048], P(None, 'frames', None, 'heads'), may hold values from -6 to 6
- value_temporal: bfloat16 [2, 16, 1024, 2048], P(None, 'frames', None, 'heads'), may hold values from -6 to 6
- output_temporal: bfloat16 [2, 16, 1024, 2048], P(None, 'frames', None, 'heads'), may hold values from -6 to 6
- grad_temporal: bfloat16 [2, 16, 1024, 2048], P(None, 'frames', None, 'heads'), may hold values from -12 to 12
Outputs:
- dquery_spatial: bfloat16 [32, 1024, 2048], P('frames', None, 'heads')
- dkey_spatial: bfloat16 [32, 1024, 2048], P('frames', None, 'heads')
- dvalue_spatial: bfloat16 [32, 1024, 2048], P('frames', None, 'heads')
- dquery_temporal: bfloat16 [2, 16, 1024, 2048], P(None, 'frames', None, 'heads')
- dkey_temporal: bfloat16 [2, 16, 1024, 2048], P(None, 'frames', None, 'heads')
- dvalue_temporal: bfloat16 [2, 16, 1024, 2048], P(None, 'frames', None, 'heads')
The draws below stay inside these ranges and needn't reach their ends.
All inputs are finite; a program needn't handle non-finite values.
Results may differ from the reference program's by a relative error of at most 0.0054.
Values may be sent and summed in bfloat16 or wider, within the bound.
A program may use at most 64 MiB of HBM per device.

```python
import jax
import jax.numpy as jnp
from jax import lax

HD = 128
P_SIZE = 1024
CLIPS = 2
HEADS = 16
FR = 32
CLIP = 16


def draw_query_spatial(key, part):
    key = jax.random.fold_in(key, 11)
    shape = (FR, P_SIZE, HEADS * HD)
    values = jax.random.truncated_normal(key, -6.0, 6.0, shape, jnp.float32)
    return values.astype(jnp.bfloat16)


def draw_key_spatial(key, part):
    key = jax.random.fold_in(key, 12)
    shape = (FR, P_SIZE, HEADS * HD)
    values = jax.random.truncated_normal(key, -6.0, 6.0, shape, jnp.float32)
    return values.astype(jnp.bfloat16)


def draw_query_temporal(key, part):
    key = jax.random.fold_in(key, 13)
    shape = (CLIPS, CLIP, P_SIZE, HEADS * HD)
    values = jax.random.truncated_normal(key, -6.0, 6.0, shape, jnp.float32)
    return values.astype(jnp.bfloat16)


def draw_key_temporal(key, part):
    key = jax.random.fold_in(key, 14)
    shape = (CLIPS, CLIP, P_SIZE, HEADS * HD)
    values = jax.random.truncated_normal(key, -6.0, 6.0, shape, jnp.float32)
    return values.astype(jnp.bfloat16)


def level_of(stream_key, extent, split, low, high):
    def one(position, blocks):
        draws = jax.random.uniform(jax.random.fold_in(jax.random.fold_in(stream_key, 6), position), (blocks,), jnp.float32, low / len(split), high / len(split))
        return jnp.repeat(jnp.exp(draws), extent[position] // blocks).reshape((-1,) + (1,) * (len(extent) - position - 1))

    gain = one(*split[0])
    for cut in split[1:]:
        gain = gain * one(*cut)
    return gain


def normal_values(stream_key, shape, width, most, split=(), kind=jnp.bfloat16):
    level = level_of(stream_key, shape, split, -0.22, 0.18) if split else 1.0
    values = jax.random.normal(stream_key, shape, jnp.float32) * width * level
    return jnp.minimum(jnp.maximum(values, -most), most).astype(kind)


def setup_inputs(seed: int = 0) -> dict:
    arg_keys = jax.random.split(jax.random.key(seed), 11)
    return {
        "query_spatial": draw_query_spatial(jax.random.fold_in(arg_keys[10], 71), 0),
        "key_spatial": draw_key_spatial(jax.random.fold_in(arg_keys[10], 71), 0),
        "value_spatial": normal_values(arg_keys[2], (FR, P_SIZE, HEADS * HD), 1.0, 6.0, ((0, 16), (2, 16))),
        "output_spatial": normal_values(arg_keys[3], (FR, P_SIZE, HEADS * HD), 1.0, 6.0, ((0, 16), (2, 16))),
        "grad_spatial": normal_values(arg_keys[4], (FR, P_SIZE, HEADS * HD), 16.0, 96.0, ((0, 16), (2, 16))),
        "query_temporal": draw_query_temporal(jax.random.fold_in(arg_keys[10], 71), 0),
        "key_temporal": draw_key_temporal(jax.random.fold_in(arg_keys[10], 71), 0),
        "value_temporal": normal_values(arg_keys[7], (CLIPS, CLIP, P_SIZE, HEADS * HD), 1.0, 6.0, ((1, 16), (3, 16))),
        "output_temporal": normal_values(arg_keys[8], (CLIPS, CLIP, P_SIZE, HEADS * HD), 1.0, 6.0, ((1, 16), (3, 16))),
        "grad_temporal": normal_values(arg_keys[9], (CLIPS, CLIP, P_SIZE, HEADS * HD), 2.0, 12.0, ((1, 16), (3, 16))),
    }


def spatial_grads(queries, key_rows, value_rows, output_rows, grad_rows):
    frames, tokens, channels = queries.shape
    head_count = channels // HD
    shape = (frames, tokens, head_count, HD)
    query_heads = queries.reshape(shape).astype(jnp.float32)
    key_heads = key_rows.reshape(shape).astype(jnp.float32)
    value_heads = value_rows.reshape(shape).astype(jnp.float32)
    output_heads = output_rows.reshape(shape).astype(jnp.float32)
    grad_heads = grad_rows.reshape(shape).astype(jnp.float32)
    scaling = HD ** -0.5
    scores = jnp.einsum("fqhd,fkhd->fhqk", query_heads, key_heads) * scaling
    weights = jax.nn.softmax(scores, axis=-1)
    weights_low = lax.optimization_barrier(weights.astype(jnp.bfloat16)).astype(jnp.float32)
    grad_value = jnp.einsum("fhqk,fqhd->fkhd", weights_low, grad_heads).astype(jnp.bfloat16)
    grad_weight = jnp.einsum("fqhd,fkhd->fhqk", grad_heads, value_heads)
    row_dot = jnp.transpose(jnp.sum(grad_heads * output_heads, axis=-1), (0, 2, 1))
    grad_score = weights * (grad_weight - row_dot[..., None])
    grad_low = lax.optimization_barrier(grad_score.astype(jnp.bfloat16)).astype(jnp.float32)
    grad_query = (jnp.einsum("fhqk,fkhd->fqhd", grad_low, key_heads) * scaling).astype(jnp.bfloat16)
    grad_key = (jnp.einsum("fhqk,fqhd->fkhd", grad_low, query_heads) * scaling).astype(jnp.bfloat16)
    final = (frames, tokens, channels)
    return grad_query.reshape(final), grad_key.reshape(final), grad_value.reshape(final)


def temporal_grads(queries, key_rows, value_rows, grad_rows, row_stats):
    clip_count, clip_len, columns, channels = queries.shape
    group = channels // HD
    shape = (clip_count, clip_len, columns, group, HD)
    query_heads = queries.reshape(shape).astype(jnp.float32)
    key_heads = key_rows.reshape(shape).astype(jnp.float32)
    value_heads = value_rows.reshape(shape).astype(jnp.float32)
    grad_heads = grad_rows.reshape(shape).astype(jnp.float32)
    scaling = HD ** -0.5
    scores = jnp.einsum("cqxyd,ckxyd->cxyqk", query_heads, key_heads) * scaling
    weights = jax.nn.softmax(scores, axis=-1)
    weights_low = lax.optimization_barrier(weights.astype(jnp.bfloat16)).astype(jnp.float32)
    grad_value = jnp.einsum("cxyqk,cqxyd->ckxyd", weights_low, grad_heads).astype(jnp.bfloat16)
    grad_weight = jnp.einsum("cqxyd,ckxyd->cxyqk", grad_heads, value_heads)
    row_dot = jnp.moveaxis(row_stats.reshape(clip_count, clip_len, columns, group).astype(jnp.float32), 1, -1)
    grad_score = weights * (grad_weight - row_dot[..., None])
    grad_low = lax.optimization_barrier(grad_score.astype(jnp.bfloat16)).astype(jnp.float32)
    grad_query = (jnp.einsum("cxyqk,ckxyd->cqxyd", grad_low, key_heads) * scaling).astype(jnp.bfloat16)
    grad_key = (jnp.einsum("cxyqk,cqxyd->ckxyd", grad_low, query_heads) * scaling).astype(jnp.bfloat16)
    final = (clip_count, clip_len, columns, channels)
    return grad_query.reshape(final), grad_key.reshape(final), grad_value.reshape(final)


def one_frame(frame_args):
    widened = tuple(piece[None] for piece in frame_args)
    results = spatial_grads(*widened)
    return tuple(piece[0] for piece in results)


def reference(query_spatial, key_spatial, value_spatial, output_spatial, grad_spatial, query_temporal, key_temporal, value_temporal, output_temporal, grad_temporal):
    dquery_s, dkey_s, dvalue_s = lax.map(one_frame, (query_spatial, key_spatial, value_spatial, output_spatial, grad_spatial))
    clip_count, clip_len, tokens, channels = query_temporal.shape
    products = grad_temporal.astype(jnp.float32) * output_temporal.astype(jnp.float32)
    row_stats = jnp.sum(products.reshape(clip_count, clip_len, tokens, channels // HD, HD), axis=-1).astype(jnp.bfloat16)
    row_stats = lax.optimization_barrier(row_stats)
    dquery_t, dkey_t, dvalue_t = temporal_grads(query_temporal, key_temporal, value_temporal, grad_temporal, row_stats)
    return (dquery_s, dkey_s, dvalue_s, dquery_t, dkey_t, dvalue_t)
```

```python
import functools
import math

import jax
import jax.numpy as jnp
from jax import lax
from jax.experimental import pallas as pl
from jax.experimental.pallas import tpu as pltpu
from jax.sharding import PartitionSpec as P

HD = 128
QB = 256
TG = 16
SCALE = HD**-0.5
EXP2_SCALE = SCALE * math.log2(math.e)


def dot(a, b, contract_a, contract_b):
    return lax.dot_general(
        a, b, (((contract_a,), (contract_b,)), ((), ())), preferred_element_type=jnp.float32
    )


def softmax(scores):
    top = jnp.max(scores, axis=-1, keepdims=True)
    powers = jnp.exp2((scores - top) * EXP2_SCALE)
    return powers * (1.0 / jnp.sum(powers, axis=-1, keepdims=True))


def kernel(
    n,
    qs_hbm, ks_hbm, vs_hbm, os_hbm, gs_hbm,
    qt_hbm, kt_hbm, vt_hbm, ot_hbm, gt_hbm,
    dqs_hbm, dks_hbm, dvs_hbm, dqt_hbm, dkt_hbm, dvt_hbm,
    spatial_in, spatial_out, dk_sum, dv_sum, stat_in, stats, stats_got, arrived, leaving,
    in_sem, out_sem, stat_in_sem, stat_send, stat_recv, go_send, go_recv, back_send, back_recv,
):
    me = lax.axis_index("frames")
    clips, _, tokens, _ = qt_hbm.shape
    part = tokens // n
    mine = pl.ds(pl.multiple_of(me * part, part), part)
    payload = (qt_hbm, kt_hbm, vt_hbm, gt_hbm)
    results = (dqt_hbm, dkt_hbm, dvt_hbm)

    def peer(step):
        return lax.rem(me + step, n)

    stat_loads = []
    for i, ref in enumerate((gt_hbm, ot_hbm)):
        copy = pltpu.make_async_copy(ref.at[:, 0], stat_in.at[i], stat_in_sem.at[i])
        copy.start()
        stat_loads.append(copy)
    loads = []
    for f in range(clips):
        group = []
        for i, ref in enumerate((qs_hbm, ks_hbm, vs_hbm, os_hbm, gs_hbm)):
            copy = pltpu.make_async_copy(ref.at[f], spatial_in.at[i, f], in_sem.at[i, f])
            copy.start()
            group.append(copy)
        loads.append(group)

    barrier = pltpu.get_barrier_semaphore()

    def greet(step, carry):
        pl.semaphore_signal(barrier, inc=1, device_id={"frames": peer(step)})
        return carry

    lax.fori_loop(1, n, greet, 0)
    pl.semaphore_wait(barrier, n - 1)

    def go(c):
        def one(step, carry):
            to = peer(step)
            rows = pl.ds(pl.multiple_of(to * part, part), part)
            for a, ref in enumerate(payload):
                pltpu.make_async_remote_copy(
                    src_ref=ref.at[c, 0, rows],
                    dst_ref=arrived.at[c, a, me],
                    send_sem=go_send.at[c],
                    recv_sem=go_recv.at[c],
                    device_id={"frames": to},
                ).start()
            return carry

        lax.fori_loop(1, n, one, 0)
        for a, ref in enumerate(payload):
            pltpu.make_async_copy(
                ref.at[c, 0, mine], arrived.at[c, a, me], go_recv.at[c]
            ).start()

    go(0)
    go(1)

    for copy in stat_loads:
        copy.wait()
    blocks = tokens // HD
    eye = lax.broadcasted_iota(jnp.int32, (HD, HD), 0) == lax.broadcasted_iota(
        jnp.int32, (HD, HD), 1
    )
    for c in range(clips):
        for b in range(blocks):
            rows = slice(b * HD, (b + 1) * HD)
            products = stat_in[0, c, rows].astype(jnp.float32) * stat_in[1, c, rows].astype(
                jnp.float32
            )
            sums = jnp.sum(products, axis=-1, keepdims=True)
            row = jnp.sum(jnp.where(eye, sums, 0.0), axis=0, keepdims=True)
            stats[b, c : c + 1] = row.astype(jnp.bfloat16).astype(jnp.float32)

    per_block = HD // part

    def send_stats(step, carry):
        to = peer(step)
        pltpu.make_async_remote_copy(
            src_ref=stats.at[to // per_block],
            dst_ref=stats_got.at[me],
            send_sem=stat_send,
            recv_sem=stat_recv,
            device_id={"frames": to},
        ).start()
        return carry

    lax.fori_loop(1, n, send_stats, 0)
    pltpu.make_async_copy(stats.at[me // per_block], stats_got.at[me], stat_recv).start()

    def spatial(f):
        for copy in loads[f]:
            copy.wait()
        keys = spatial_in[1, f]
        values = spatial_in[2, f]
        for i in range(tokens // QB):
            rows = slice(i * QB, (i + 1) * QB)
            query = spatial_in[0, f, rows]
            grad = spatial_in[4, f, rows]
            rowdot = jnp.sum(
                grad.astype(jnp.float32) * spatial_in[3, f, rows].astype(jnp.float32),
                axis=-1,
                keepdims=True,
            )
            weights = softmax(dot(query, keys, 1, 1))
            dweights = dot(grad, values, 1, 1)
            dscores = (weights * (dweights - rowdot)).astype(jnp.bfloat16)
            dv = dot(weights.astype(jnp.bfloat16), grad, 0, 0)
            dk = dot(dscores, query, 0, 0)
            if i:
                dv = dv + dv_sum[...]
                dk = dk + dk_sum[...]
            if i < tokens // QB - 1:
                dv_sum[...] = dv
                dk_sum[...] = dk
            else:
                spatial_out[2, f] = dv.astype(jnp.bfloat16)
                spatial_out[1, f] = (dk * SCALE).astype(jnp.bfloat16)
            spatial_out[0, f, rows] = (dot(dscores, keys, 1, 0) * SCALE).astype(jnp.bfloat16)
        copies = []
        for i, ref in enumerate((dqs_hbm, dks_hbm, dvs_hbm)):
            copy = pltpu.make_async_copy(spatial_out.at[i, f], ref.at[f], out_sem.at[i, f])
            copy.start()
            copies.append(copy)
        return copies

    side = n * TG
    same_token = (
        lax.broadcasted_iota(jnp.int32, (side, side), 0) % TG
        == lax.broadcasted_iota(jnp.int32, (side, side), 1) % TG
    )

    def temporal(c):
        pltpu.make_async_copy(arrived.at[c], arrived.at[c], go_recv.at[c]).wait()
        if c == 0:
            pltpu.make_async_copy(stats_got, stats_got, stat_recv).wait()
        row_stats = (
            jnp.broadcast_to(stats_got[:, c : c + 1], (n, TG, HD))
            .reshape(side, HD)
            .astype(jnp.bfloat16)
        )
        lane = lax.broadcasted_iota(jnp.int32, (side, HD), 1)
        token = lax.broadcasted_iota(jnp.int32, (side, HD), 0) % TG
        first = lax.rem(me, per_block) * part
        for g in range(part // TG):
            rows = slice(g * TG, (g + 1) * TG)
            query = arrived[c, 0, :, rows].reshape(side, HD)
            keys = arrived[c, 1, :, rows].reshape(side, HD)
            values = arrived[c, 2, :, rows].reshape(side, HD)
            grad = arrived[c, 3, :, rows].reshape(side, HD)
            pick = jnp.where(lane == first + g * TG + token, -1.0, 0.0).astype(jnp.bfloat16)
            weights = softmax(jnp.where(same_token, dot(query, keys, 1, 1), -1e30))
            shifted = dot(grad, values, 1, 1) + dot(row_stats, pick, 1, 1)
            dscores = (weights * shifted).astype(jnp.bfloat16)
            dv = dot(weights.astype(jnp.bfloat16), grad, 0, 0)
            dq = dot(dscores, keys, 1, 0) * SCALE
            dk = dot(dscores, query, 0, 0) * SCALE
            for a, value in enumerate((dq, dk, dv)):
                leaving[c, a, :, rows] = value.astype(jnp.bfloat16).reshape(n, TG, HD)

        def one(step, carry):
            to = peer(step)
            for a, ref in enumerate(results):
                pltpu.make_async_remote_copy(
                    src_ref=leaving.at[c, a, to],
                    dst_ref=ref.at[c, 0, mine],
                    send_sem=back_send.at[a],
                    recv_sem=back_recv.at[a],
                    device_id={"frames": to},
                ).start()
            return carry

        lax.fori_loop(1, n, one, 0)
        for a, ref in enumerate(results):
            pltpu.make_async_copy(
                leaving.at[c, a, me], ref.at[c, 0, mine], back_recv.at[a]
            ).start()

    copies = spatial(0)
    temporal(0)
    copies += spatial(1)
    temporal(1)

    for copy in copies:
        copy.wait()
    for c in range(clips):
        sent = arrived.at[c, :, pl.ds(0, n - 1)]
        pltpu.make_async_copy(sent, sent, go_send.at[c]).wait()
    sent = stats_got.at[pl.ds(0, n - 1)]
    pltpu.make_async_copy(sent, sent, stat_send).wait()
    for a, ref in enumerate(results):
        sent = leaving.at[:, a, pl.ds(0, n - 1)]
        pltpu.make_async_copy(sent, sent, back_send.at[a]).wait()
        pltpu.make_async_copy(ref, ref, back_recv.at[a]).wait()


def body(*args):
    n = lax.axis_size("frames")
    spatial, temporal = args[0], args[5]
    frames, tokens, _ = spatial.shape
    clips = temporal.shape[0]
    part = tokens // n
    hbm = pl.BlockSpec(memory_space=pltpu.HBM)
    out_shape = [jax.ShapeDtypeStruct(spatial.shape, jnp.bfloat16)] * 3 + [
        jax.ShapeDtypeStruct(temporal.shape, jnp.bfloat16)
    ] * 3
    dma = pltpu.SemaphoreType.DMA
    return tuple(
        pl.pallas_call(
            functools.partial(kernel, n),
            out_shape=out_shape,
            in_specs=[hbm] * 10,
            out_specs=[hbm] * 6,
            scratch_shapes=[
                pltpu.VMEM((5, frames, tokens, HD), jnp.bfloat16),
                pltpu.VMEM((3, frames, tokens, HD), jnp.bfloat16),
                pltpu.VMEM((tokens, HD), jnp.float32),
                pltpu.VMEM((tokens, HD), jnp.float32),
                pltpu.VMEM((2, clips, tokens, HD), jnp.bfloat16),
                pltpu.VMEM((tokens // HD, clips, HD), jnp.float32),
                pltpu.VMEM((n, clips, HD), jnp.float32),
                pltpu.VMEM((clips, 4, n, part, HD), jnp.bfloat16),
                pltpu.VMEM((clips, 3, n, part, HD), jnp.bfloat16),
                dma((5, frames)),
                dma((3, frames)),
                dma((2,)),
                dma,
                dma,
                dma((clips,)),
                dma((clips,)),
                dma((3,)),
                dma((3,)),
            ],
            compiler_params=pltpu.CompilerParams(
                collective_id=0, has_side_effects=True, vmem_limit_bytes=56 * 2**20
            ),
            cost_estimate=pl.CostEstimate(
                flops=5 * 2 * frames * tokens * tokens * HD,
                bytes_accessed=16 * frames * tokens * HD * 2,
                transcendentals=frames * tokens * tokens,
            ),
        )(*args)
    )


def solution(mesh):
    spatial = P("frames", None, "heads")
    temporal = P(None, "frames", None, "heads")
    return jax.shard_map(
        body,
        mesh=mesh,
        in_specs=(spatial,) * 5 + (temporal,) * 5,
        out_specs=(spatial,) * 3 + (temporal,) * 3,
        check_vma=False,
    )
```

```python
import functools
import math

import jax
import jax.numpy as jnp
from jax import lax
from jax.experimental import pallas as pl
from jax.experimental.pallas import tpu as pltpu
from jax.sharding import PartitionSpec as P

HD = 128
QB = 256
TG = 16
SCALE = HD**-0.5
STEPS = (
    (1, 2, 0), (1, 2, 1), (1, 1, 0), (1, 3, 1), (1, 3, 0), (1, 1, 1), (0, 2, 0), (1, 0, 1),
    (0, 2, 1), (1, 0, 0), (0, 1, 0), (0, 3, 1), (0, 3, 0), (0, 1, 1), (0, 0, 1),
)
EXP2_SCALE = SCALE * math.log2(math.e)


def dot(a, b, contract_a, contract_b):
    return lax.dot_general(
        a, b, (((contract_a,), (contract_b,)), ((), ())), preferred_element_type=jnp.float32
    )


def softmax(scores):
    top = jnp.max(scores, axis=-1, keepdims=True)
    powers = jnp.exp2((scores - top) * EXP2_SCALE)
    return powers * (1.0 / jnp.sum(powers, axis=-1, keepdims=True))


def kernel(
    n,
    qs_hbm, ks_hbm, vs_hbm, os_hbm, gs_hbm,
    qt_hbm, kt_hbm, vt_hbm, ot_hbm, gt_hbm,
    dqs_hbm, dks_hbm, dvs_hbm, dqt_hbm, dkt_hbm, dvt_hbm,
    spatial_in, spatial_out, dk_sum, dv_sum, stat_in, stats, stats_got, arrived, leaving,
    in_sem, out_sem, stat_in_sem, stat_send, stat_recv, go_send, go_recv, back_send, back_recv,
):
    me = lax.axis_index("frames")
    clips, _, tokens, _ = qt_hbm.shape
    part = tokens // n
    mine = pl.ds(pl.multiple_of(me * part, part), part)
    payload = (qt_hbm, kt_hbm, vt_hbm, gt_hbm)
    results = (dqt_hbm, dkt_hbm, dvt_hbm)

    z, y, core = me // 8, lax.rem(me // 2, 4), lax.rem(me, 2)
    peers = [
        lax.rem(z + dz, 2) * 8 + lax.rem(y + dy, 4) * 2 + lax.rem(core + dc, 2)
        for dz, dy, dc in STEPS
    ]

    stat_loads = []
    for i, ref in enumerate((gt_hbm, ot_hbm)):
        copy = pltpu.make_async_copy(ref.at[:, 0], stat_in.at[i], stat_in_sem.at[i])
        copy.start()
        stat_loads.append(copy)
    loads = []
    for f in range(clips):
        group = []
        for i, ref in enumerate((qs_hbm, ks_hbm, vs_hbm, os_hbm, gs_hbm)):
            copy = pltpu.make_async_copy(ref.at[f], spatial_in.at[i, f], in_sem.at[i, f])
            copy.start()
            group.append(copy)
        loads.append(group)

    barrier = pltpu.get_barrier_semaphore()

    for to in peers:
        pl.semaphore_signal(barrier, inc=1, device_id={"frames": to})
    pl.semaphore_wait(barrier, n - 1)

    def go(c):
        for a, ref in enumerate(payload):
            for to in peers:
                rows = pl.ds(pl.multiple_of(to * part, part), part)
                pltpu.make_async_remote_copy(
                    src_ref=ref.at[c, 0, rows],
                    dst_ref=arrived.at[c, a, me],
                    send_sem=go_send.at[c],
                    recv_sem=go_recv.at[c],
                    device_id={"frames": to},
                ).start()
            pltpu.make_async_copy(
                ref.at[c, 0, mine], arrived.at[c, a, me], go_recv.at[c]
            ).start()

    go(0)

    for copy in stat_loads:
        copy.wait()
    blocks = tokens // HD
    eye = lax.broadcasted_iota(jnp.int32, (HD, HD), 0) == lax.broadcasted_iota(
        jnp.int32, (HD, HD), 1
    )
    for c in range(clips):
        for b in range(blocks):
            rows = slice(b * HD, (b + 1) * HD)
            products = stat_in[0, c, rows].astype(jnp.float32) * stat_in[1, c, rows].astype(
                jnp.float32
            )
            sums = jnp.sum(products, axis=-1, keepdims=True)
            row = jnp.sum(jnp.where(eye, sums, 0.0), axis=0, keepdims=True)
            stats[b, c : c + 1] = row.astype(jnp.bfloat16).astype(jnp.float32)

    per_block = HD // part

    for to in peers:
        pltpu.make_async_remote_copy(
            src_ref=stats.at[to // per_block],
            dst_ref=stats_got.at[me],
            send_sem=stat_send,
            recv_sem=stat_recv,
            device_id={"frames": to},
        ).start()
    pltpu.make_async_copy(stats.at[me // per_block], stats_got.at[me], stat_recv).start()

    for c in range(1, clips):
        go(c)

    def spatial(f):
        for copy in loads[f]:
            copy.wait()
        keys = spatial_in[1, f]
        values = spatial_in[2, f]
        for i in range(tokens // QB):
            rows = slice(i * QB, (i + 1) * QB)
            query = spatial_in[0, f, rows]
            grad = spatial_in[4, f, rows]
            rowdot = jnp.sum(
                grad.astype(jnp.float32) * spatial_in[3, f, rows].astype(jnp.float32),
                axis=-1,
                keepdims=True,
            )
            weights = softmax(dot(query, keys, 1, 1))
            dweights = dot(grad, values, 1, 1)
            dscores = (weights * (dweights - rowdot)).astype(jnp.bfloat16)
            dv = dot(weights.astype(jnp.bfloat16), grad, 0, 0)
            dk = dot(dscores, query, 0, 0)
            if i:
                dv = dv + dv_sum[...]
                dk = dk + dk_sum[...]
            if i < tokens // QB - 1:
                dv_sum[...] = dv
                dk_sum[...] = dk
            else:
                spatial_out[2, f] = dv.astype(jnp.bfloat16)
                spatial_out[1, f] = (dk * SCALE).astype(jnp.bfloat16)
            spatial_out[0, f, rows] = (dot(dscores, keys, 1, 0) * SCALE).astype(jnp.bfloat16)
        copies = []
        for i, ref in enumerate((dqs_hbm, dks_hbm, dvs_hbm)):
            copy = pltpu.make_async_copy(spatial_out.at[i, f], ref.at[f], out_sem.at[i, f])
            copy.start()
            copies.append(copy)
        return copies

    side = n * TG
    same_token = (
        lax.broadcasted_iota(jnp.int32, (side, side), 0) % TG
        == lax.broadcasted_iota(jnp.int32, (side, side), 1) % TG
    )

    def temporal(c):
        pltpu.make_async_copy(arrived.at[c], arrived.at[c], go_recv.at[c]).wait()
        if c == 0:
            pltpu.make_async_copy(stats_got, stats_got, stat_recv).wait()
        row_stats = (
            jnp.broadcast_to(stats_got[:, c : c + 1], (n, TG, HD))
            .reshape(side, HD)
            .astype(jnp.bfloat16)
        )
        lane = lax.broadcasted_iota(jnp.int32, (side, HD), 1)
        token = lax.broadcasted_iota(jnp.int32, (side, HD), 0) % TG
        first = lax.rem(me, per_block) * part
        for g in range(part // TG):
            rows = slice(g * TG, (g + 1) * TG)
            query = arrived[c, 0, :, rows].reshape(side, HD)
            keys = arrived[c, 1, :, rows].reshape(side, HD)
            values = arrived[c, 2, :, rows].reshape(side, HD)
            grad = arrived[c, 3, :, rows].reshape(side, HD)
            pick = jnp.where(lane == first + g * TG + token, -1.0, 0.0).astype(jnp.bfloat16)
            weights = softmax(jnp.where(same_token, dot(query, keys, 1, 1), -1e30))
            shifted = dot(grad, values, 1, 1) + dot(row_stats, pick, 1, 1)
            dscores = (weights * shifted).astype(jnp.bfloat16)
            dv = dot(weights.astype(jnp.bfloat16), grad, 0, 0)
            dq = dot(dscores, keys, 1, 0) * SCALE
            dk = dot(dscores, query, 0, 0) * SCALE
            for a, value in enumerate((dq, dk, dv)):
                leaving[c, a, :, rows] = value.astype(jnp.bfloat16).reshape(n, TG, HD)

        for a, ref in enumerate(results):
            for to in peers:
                pltpu.make_async_remote_copy(
                    src_ref=leaving.at[c, a, to],
                    dst_ref=ref.at[c, 0, mine],
                    send_sem=back_send.at[a],
                    recv_sem=back_recv.at[a],
                    device_id={"frames": to},
                ).start()
            pltpu.make_async_copy(
                leaving.at[c, a, me], ref.at[c, 0, mine], back_recv.at[a]
            ).start()

    copies = spatial(0)
    temporal(0)
    copies += spatial(1)
    temporal(1)

    for copy in copies:
        copy.wait()
    for c in range(clips):
        sent = arrived.at[c, :, pl.ds(0, n - 1)]
        pltpu.make_async_copy(sent, sent, go_send.at[c]).wait()
    sent = stats_got.at[pl.ds(0, n - 1)]
    pltpu.make_async_copy(sent, sent, stat_send).wait()
    for a, ref in enumerate(results):
        sent = leaving.at[:, a, pl.ds(0, n - 1)]
        pltpu.make_async_copy(sent, sent, back_send.at[a]).wait()
        pltpu.make_async_copy(ref, ref, back_recv.at[a]).wait()


def write_out(*refs):
    sources, targets = refs[:6], refs[6:12]
    held, in_sem, out_sem = refs[12:]
    halves = held.shape[1]
    jobs = []
    for h in range(halves):
        for i in range(6):
            load = pltpu.make_async_copy(sources[i].at[h], held.at[i, h], in_sem.at[i, h])
            load.start()
            store = pltpu.make_async_copy(held.at[i, h], targets[i].at[h], out_sem.at[i, h])
            jobs.append((load, store))
    for load, store in jobs:
        load.wait()
        store.start()
    for load, store in jobs:
        store.wait()


def body(*args):
    n = lax.axis_size("frames")
    spatial, temporal = args[0], args[5]
    frames, tokens, _ = spatial.shape
    clips = temporal.shape[0]
    part = tokens // n
    hbm = pl.BlockSpec(memory_space=pltpu.HBM)
    out_shape = [jax.ShapeDtypeStruct(spatial.shape, jnp.bfloat16)] * 3 + [
        jax.ShapeDtypeStruct(temporal.shape, jnp.bfloat16)
    ] * 3
    dma = pltpu.SemaphoreType.DMA
    gradients = pl.pallas_call(
        functools.partial(kernel, n),
        out_shape=out_shape,
        in_specs=[hbm] * 10,
        out_specs=[hbm] * 6,
        scratch_shapes=[
            pltpu.VMEM((5, frames, tokens, HD), jnp.bfloat16),
            pltpu.VMEM((3, frames, tokens, HD), jnp.bfloat16),
            pltpu.VMEM((tokens, HD), jnp.float32),
            pltpu.VMEM((tokens, HD), jnp.float32),
            pltpu.VMEM((2, clips, tokens, HD), jnp.bfloat16),
            pltpu.VMEM((tokens // HD, clips, HD), jnp.float32),
            pltpu.VMEM((n, clips, HD), jnp.float32),
            pltpu.VMEM((clips, 4, n, part, HD), jnp.bfloat16),
            pltpu.VMEM((clips, 3, n, part, HD), jnp.bfloat16),
            dma((5, frames)),
            dma((3, frames)),
            dma((2,)),
            dma,
            dma,
            dma((clips,)),
            dma((clips,)),
            dma((3,)),
            dma((3,)),
        ],
        compiler_params=pltpu.CompilerParams(
            collective_id=0, has_side_effects=True, vmem_limit_bytes=56 * 2**20
        ),
        cost_estimate=pl.CostEstimate(
            flops=5 * 2 * frames * tokens * tokens * HD,
            bytes_accessed=16 * frames * tokens * HD * 2,
            transcendentals=frames * tokens * tokens,
        ),
    )(*args)
    flat = [g.reshape(spatial.shape) for g in gradients]
    written = pl.pallas_call(
        write_out,
        out_shape=out_shape[:1] * 6,
        in_specs=[hbm] * 6,
        out_specs=[hbm] * 6,
        scratch_shapes=[
            pltpu.VMEM((6, frames, tokens, HD), jnp.bfloat16),
            dma((6, frames)),
            dma((6, frames)),
        ],
    )(*flat)
    return tuple(g.reshape(o.shape) for o, g in zip(out_shape, written))


def solution(mesh):
    spatial = P("frames", None, "heads")
    temporal = P(None, "frames", None, "heads")
    return jax.shard_map(
        body,
        mesh=mesh,
        in_specs=(spatial,) * 5 + (temporal,) * 5,
        out_specs=(spatial,) * 3 + (temporal,) * 3,
        check_vma=False,
    )
```

```python
import functools
import math

import jax
import jax.numpy as jnp
from jax import lax
from jax.experimental import pallas as pl
from jax.experimental.pallas import tpu as pltpu
from jax.sharding import PartitionSpec as P

HD = 128
QB = 256
TG = 16
VMEM_LIMIT = 101 * 2**19
SCALE = HD**-0.5
STEPS = (
    (1, 2, 0), (1, 2, 1), (1, 1, 0), (1, 3, 1), (1, 3, 0), (1, 1, 1), (0, 2, 0), (1, 0, 1),
    (0, 2, 1), (1, 0, 0), (0, 1, 0), (0, 3, 1), (0, 3, 0), (0, 1, 1), (0, 0, 1),
)
EXP2_SCALE = SCALE * math.log2(math.e)


def dot(a, b, contract_a, contract_b):
    return lax.dot_general(
        a, b, (((contract_a,), (contract_b,)), ((), ())), preferred_element_type=jnp.float32
    )


def softmax(scores):
    top = jnp.max(scores, axis=-1, keepdims=True)
    powers = jnp.exp2((scores - top) * EXP2_SCALE)
    return powers * (1.0 / jnp.sum(powers, axis=-1, keepdims=True))


def kernel(
    n,
    qs_hbm, ks_hbm, vs_hbm, os_hbm, gs_hbm,
    qt_hbm, kt_hbm, vt_hbm, ot_hbm, gt_hbm,
    dqs_hbm, dks_hbm, dvs_hbm, dqt_hbm, dkt_hbm, dvt_hbm,
    spatial_in, spatial_out, dk_sum, dv_sum, stat_in, stats, stats_got, arrived, leaving,
    in_sem, out_sem, stat_in_sem, stat_send, stat_recv, go_send, go_recv, back_send, back_recv,
):
    me = lax.axis_index("frames")
    clips, _, tokens, _ = qt_hbm.shape
    part = tokens // n
    mine = pl.ds(pl.multiple_of(me * part, part), part)
    payload = (qt_hbm, kt_hbm, vt_hbm, gt_hbm)
    results = (dqt_hbm, dkt_hbm, dvt_hbm)

    z, y, core = me // 8, lax.rem(me // 2, 4), lax.rem(me, 2)
    peers = [
        lax.rem(z + dz, 2) * 8 + lax.rem(y + dy, 4) * 2 + lax.rem(core + dc, 2)
        for dz, dy, dc in STEPS
    ]

    barrier = pltpu.get_barrier_semaphore()
    for to in peers:
        pl.semaphore_signal(barrier, inc=1, device_id={"frames": to})

    stat_loads = []
    for i, ref in enumerate((gt_hbm, ot_hbm)):
        copy = pltpu.make_async_copy(ref.at[:, 0], stat_in.at[i], stat_in_sem.at[i])
        copy.start()
        stat_loads.append(copy)
    loads = []
    for f in range(clips):
        group = []
        for i, ref in enumerate((qs_hbm, ks_hbm, vs_hbm, os_hbm, gs_hbm)):
            copy = pltpu.make_async_copy(ref.at[f], spatial_in.at[i, f], in_sem.at[i, f])
            copy.start()
            group.append(copy)
        loads.append(group)

    pl.semaphore_wait(barrier, n - 1)

    def go(c):
        for a, ref in enumerate(payload):
            for to in peers:
                rows = pl.ds(pl.multiple_of(to * part, part), part)
                pltpu.make_async_remote_copy(
                    src_ref=ref.at[c, 0, rows],
                    dst_ref=arrived.at[c, a, me],
                    send_sem=go_send.at[c],
                    recv_sem=go_recv.at[c],
                    device_id={"frames": to},
                ).start()
            pltpu.make_async_copy(
                ref.at[c, 0, mine], arrived.at[c, a, me], go_recv.at[c]
            ).start()

    go(0)

    for copy in stat_loads:
        copy.wait()
    blocks = tokens // HD
    eye = lax.broadcasted_iota(jnp.int32, (HD, HD), 0) == lax.broadcasted_iota(
        jnp.int32, (HD, HD), 1
    )
    for c in range(clips):
        for b in range(blocks):
            rows = slice(b * HD, (b + 1) * HD)
            products = stat_in[0, c, rows].astype(jnp.float32) * stat_in[1, c, rows].astype(
                jnp.float32
            )
            sums = jnp.sum(products, axis=-1, keepdims=True)
            row = jnp.sum(jnp.where(eye, sums, 0.0), axis=0, keepdims=True)
            stats[b, c : c + 1] = row.astype(jnp.bfloat16).astype(jnp.float32)

    per_block = HD // part

    for to in peers:
        pltpu.make_async_remote_copy(
            src_ref=stats.at[to // per_block],
            dst_ref=stats_got.at[me],
            send_sem=stat_send,
            recv_sem=stat_recv,
            device_id={"frames": to},
        ).start()
    pltpu.make_async_copy(stats.at[me // per_block], stats_got.at[me], stat_recv).start()

    for c in range(1, clips):
        go(c)

    def spatial(f):
        for copy in loads[f]:
            copy.wait()
        keys = spatial_in[1, f]
        values = spatial_in[2, f]
        for i in range(tokens // QB):
            rows = slice(i * QB, (i + 1) * QB)
            query = spatial_in[0, f, rows]
            grad = spatial_in[4, f, rows]
            rowdot = jnp.sum(
                grad.astype(jnp.float32) * spatial_in[3, f, rows].astype(jnp.float32),
                axis=-1,
                keepdims=True,
            )
            weights = softmax(dot(query, keys, 1, 1))
            dweights = dot(grad, values, 1, 1)
            dscores = (weights * (dweights - rowdot)).astype(jnp.bfloat16)
            dv = dot(weights.astype(jnp.bfloat16), grad, 0, 0)
            dk = dot(dscores, query, 0, 0)
            if i:
                dv = dv + dv_sum[...]
                dk = dk + dk_sum[...]
            if i < tokens // QB - 1:
                dv_sum[...] = dv
                dk_sum[...] = dk
            else:
                spatial_out[2, f] = dv.astype(jnp.bfloat16)
                spatial_out[1, f] = (dk * SCALE).astype(jnp.bfloat16)
            spatial_out[0, f, rows] = (dot(dscores, keys, 1, 0) * SCALE).astype(jnp.bfloat16)
        copies = []
        for i, ref in enumerate((dqs_hbm, dks_hbm, dvs_hbm)):
            copy = pltpu.make_async_copy(spatial_out.at[i, f], ref.at[f], out_sem.at[i, f])
            copy.start()
            copies.append(copy)
        return copies

    side = n * TG
    same_token = (
        lax.broadcasted_iota(jnp.int32, (side, side), 0) % TG
        == lax.broadcasted_iota(jnp.int32, (side, side), 1) % TG
    )

    def temporal(c):
        pltpu.make_async_copy(arrived.at[c], arrived.at[c], go_recv.at[c]).wait()
        if c == 0:
            pltpu.make_async_copy(stats_got, stats_got, stat_recv).wait()
        row_stats = (
            jnp.broadcast_to(stats_got[:, c : c + 1], (n, TG, HD))
            .reshape(side, HD)
            .astype(jnp.bfloat16)
        )
        lane = lax.broadcasted_iota(jnp.int32, (side, HD), 1)
        token = lax.broadcasted_iota(jnp.int32, (side, HD), 0) % TG
        first = lax.rem(me, per_block) * part
        for g in range(part // TG):
            rows = slice(g * TG, (g + 1) * TG)
            query = arrived[c, 0, :, rows].reshape(side, HD)
            keys = arrived[c, 1, :, rows].reshape(side, HD)
            values = arrived[c, 2, :, rows].reshape(side, HD)
            grad = arrived[c, 3, :, rows].reshape(side, HD)
            pick = jnp.where(lane == first + g * TG + token, -1.0, 0.0).astype(jnp.bfloat16)
            weights = softmax(jnp.where(same_token, dot(query, keys, 1, 1), -1e30))
            shifted = dot(grad, values, 1, 1) + dot(row_stats, pick, 1, 1)
            dscores = (weights * shifted).astype(jnp.bfloat16)
            dv = dot(weights.astype(jnp.bfloat16), grad, 0, 0)
            dq = dot(dscores, keys, 1, 0) * SCALE
            dk = dot(dscores, query, 0, 0) * SCALE
            for a, value in enumerate((dq, dk, dv)):
                leaving[c, a, :, rows] = value.astype(jnp.bfloat16).reshape(n, TG, HD)

        for a, ref in enumerate(results):
            for to in peers:
                pltpu.make_async_remote_copy(
                    src_ref=leaving.at[c, a, to],
                    dst_ref=ref.at[c, 0, mine],
                    send_sem=back_send.at[a],
                    recv_sem=back_recv.at[a],
                    device_id={"frames": to},
                ).start()
            pltpu.make_async_copy(
                leaving.at[c, a, me], ref.at[c, 0, mine], back_recv.at[a]
            ).start()

    copies = spatial(0)
    temporal(0)
    copies += spatial(1)
    temporal(1)

    for copy in copies:
        copy.wait()
    for c in range(clips):
        sent = arrived.at[c, :, pl.ds(0, n - 1)]
        pltpu.make_async_copy(sent, sent, go_send.at[c]).wait()
    sent = stats_got.at[pl.ds(0, n - 1)]
    pltpu.make_async_copy(sent, sent, stat_send).wait()
    for a, ref in enumerate(results):
        sent = leaving.at[:, a, pl.ds(0, n - 1)]
        pltpu.make_async_copy(sent, sent, back_send.at[a]).wait()
        pltpu.make_async_copy(ref, ref, back_recv.at[a]).wait()


def write_out(*refs):
    sources, targets, sem = refs[:6], refs[6:12], refs[12]
    copies = [pltpu.make_async_copy(sources[i], targets[i], sem.at[i]) for i in range(6)]
    for copy in copies:
        copy.start()
    for copy in copies:
        copy.wait()


def body(*args):
    n = lax.axis_size("frames")
    spatial, temporal = args[0], args[5]
    frames, tokens, _ = spatial.shape
    clips = temporal.shape[0]
    part = tokens // n
    hbm = pl.BlockSpec(memory_space=pltpu.HBM)
    anywhere = pl.BlockSpec(memory_space=pl.ANY)
    out_shape = [jax.ShapeDtypeStruct(spatial.shape, jnp.bfloat16)] * 3 + [
        jax.ShapeDtypeStruct(temporal.shape, jnp.bfloat16)
    ] * 3
    dma = pltpu.SemaphoreType.DMA
    gradients = pl.pallas_call(
        functools.partial(kernel, n),
        out_shape=out_shape,
        in_specs=[hbm] * 10,
        out_specs=[anywhere] * 6,
        scratch_shapes=[
            pltpu.VMEM((5, frames, tokens, HD), jnp.bfloat16),
            pltpu.VMEM((3, frames, tokens, HD), jnp.bfloat16),
            pltpu.VMEM((tokens, HD), jnp.float32),
            pltpu.VMEM((tokens, HD), jnp.float32),
            pltpu.VMEM((2, clips, tokens, HD), jnp.bfloat16),
            pltpu.VMEM((tokens // HD, clips, HD), jnp.float32),
            pltpu.VMEM((n, clips, HD), jnp.float32),
            pltpu.VMEM((clips, 4, n, part, HD), jnp.bfloat16),
            pltpu.VMEM((clips, 3, n, part, HD), jnp.bfloat16),
            dma((5, frames)),
            dma((3, frames)),
            dma((2,)),
            dma,
            dma,
            dma((clips,)),
            dma((clips,)),
            dma((3,)),
            dma((3,)),
        ],
        compiler_params=pltpu.CompilerParams(
            collective_id=0, has_side_effects=True, vmem_limit_bytes=VMEM_LIMIT
        ),
        cost_estimate=pl.CostEstimate(
            flops=5 * 2 * frames * tokens * tokens * HD,
            bytes_accessed=16 * frames * tokens * HD * 2,
            transcendentals=frames * tokens * tokens,
        ),
    )(*args)
    flat = [g.reshape(spatial.shape) for g in gradients]
    written = pl.pallas_call(
        write_out,
        out_shape=out_shape[:1] * 6,
        in_specs=[anywhere] * 6,
        out_specs=[hbm] * 6,
        scratch_shapes=[dma((6,))],
        compiler_params=pltpu.CompilerParams(vmem_limit_bytes=2 * 2**20),
    )(*flat)
    return tuple(g.reshape(o.shape) for o, g in zip(out_shape, written))


def solution(mesh):
    spatial = P("frames", None, "heads")
    temporal = P(None, "frames", None, "heads")
    return jax.shard_map(
        body,
        mesh=mesh,
        in_specs=(spatial,) * 5 + (temporal,) * 5,
        out_specs=(spatial,) * 3 + (temporal,) * 3,
        check_vma=False,
    )
```

```python
import functools
import math

import jax
import jax.numpy as jnp
from jax import lax
from jax.experimental import pallas as pl
from jax.experimental.pallas import tpu as pltpu
from jax.sharding import PartitionSpec as P

HD = 128
QB = 256
TG = 16
VMEM_LIMIT = 101 * 2**19
SCALE = HD**-0.5
NEAR = ((1, 0, 0), (0, 1, 0), (0, 3, 0), (1, 0, 1), (0, 1, 1), (0, 3, 1), (0, 0, 1))
MIDDLE = ((0, 2, 0), (1, 1, 0), (1, 3, 0), (0, 2, 1), (1, 1, 1), (1, 3, 1))
FAR = ((1, 2, 0), (1, 2, 1))
VMEM_LIMIT = 101 * 2**19
SCALE = HD**-0.5
STEPS = (
    (1, 2, 0), (1, 2, 1), (1, 1, 0), (1, 3, 1), (1, 3, 0), (1, 1, 1), (0, 2, 0), (1, 0, 1),
    (0, 2, 1), (1, 0, 0), (0, 1, 0), (0, 3, 1), (0, 3, 0), (0, 1, 1), (0, 0, 1),
)
EXP2_SCALE = SCALE * math.log2(math.e)


def dot(a, b, contract_a, contract_b):
    return lax.dot_general(
        a, b, (((contract_a,), (contract_b,)), ((), ())), preferred_element_type=jnp.float32
    )


def softmax(scores):
    top = jnp.max(scores, axis=-1, keepdims=True)
    powers = jnp.exp2((scores - top) * EXP2_SCALE)
    return powers * (1.0 / jnp.sum(powers, axis=-1, keepdims=True))


def kernel(
    n,
    qs_hbm, ks_hbm, vs_hbm, os_hbm, gs_hbm,
    qt_hbm, kt_hbm, vt_hbm, ot_hbm, gt_hbm,
    dqs_hbm, dks_hbm, dvs_hbm, dqt_hbm, dkt_hbm, dvt_hbm,
    spatial_in, spatial_out, dk_sum, dv_sum, stat_in, stats, stats_got, arrived, leaving,
    in_sem, out_sem, stat_in_sem, stat_send, stat_recv, go_send, go_recv, back_send, back_recv,
    near_sem, middle_sem,
):
    me = lax.axis_index("frames")
    clips, _, tokens, _ = qt_hbm.shape
    part = tokens // n
    mine = pl.ds(pl.multiple_of(me * part, part), part)
    payload = (qt_hbm, kt_hbm, vt_hbm, gt_hbm)
    results = (dqt_hbm, dkt_hbm, dvt_hbm)

    z, y, core = me // 8, lax.rem(me // 2, 4), lax.rem(me, 2)

    def at(step):
        dz, dy, dc = step
        return lax.rem(z + dz, 2) * 8 + lax.rem(y + dy, 4) * 2 + lax.rem(core + dc, 2)

    near, middle, far = ([at(step) for step in steps] for steps in (NEAR, MIDDLE, FAR))
    everyone = far + middle + near

    barrier = pltpu.get_barrier_semaphore()
    for to in near:
        pl.semaphore_signal(barrier, inc=1, device_id={"frames": to})

    def go(c, peers):
        for a, ref in enumerate(payload):
            for to in peers:
                rows = pl.ds(pl.multiple_of(to * part, part), part)
                pltpu.make_async_remote_copy(
                    src_ref=ref.at[c, 0, rows],
                    dst_ref=arrived.at[c, a, me],
                    send_sem=go_send.at[c],
                    recv_sem=go_recv.at[c],
                    device_id={"frames": to},
                ).start()

    def stay(c):
        for a, ref in enumerate(payload):
            pltpu.make_async_copy(
                ref.at[c, 0, mine], arrived.at[c, a, me], go_recv.at[c]
            ).start()

    pl.semaphore_wait(barrier, len(NEAR))
    for step in NEAR[:3]:
        pl.semaphore_signal(near_sem, inc=1, device_id={"frames": at(step)})
    go(0, near)

    stat_loads = []
    for i, ref in enumerate((gt_hbm, ot_hbm)):
        copy = pltpu.make_async_copy(ref.at[:, 0], stat_in.at[i], stat_in_sem.at[i])
        copy.start()
        stat_loads.append(copy)
    loads = []
    for f in range(clips):
        group = []
        for i, ref in enumerate((qs_hbm, ks_hbm, vs_hbm, os_hbm, gs_hbm)):
            copy = pltpu.make_async_copy(ref.at[f], spatial_in.at[i, f], in_sem.at[i, f])
            copy.start()
            group.append(copy)
        loads.append(group)

    stay(0)
    pl.semaphore_wait(near_sem, 3)
    pl.semaphore_signal(middle_sem, inc=1, device_id={"frames": at(NEAR[0])})
    go(0, middle)
    pl.semaphore_wait(middle_sem, 1)
    go(0, far)

    for copy in stat_loads:
        copy.wait()
    blocks = tokens // HD
    eye = lax.broadcasted_iota(jnp.int32, (HD, HD), 0) == lax.broadcasted_iota(
        jnp.int32, (HD, HD), 1
    )
    for c in range(clips):
        for b in range(blocks):
            rows = slice(b * HD, (b + 1) * HD)
            products = stat_in[0, c, rows].astype(jnp.float32) * stat_in[1, c, rows].astype(
                jnp.float32
            )
            sums = jnp.sum(products, axis=-1, keepdims=True)
            row = jnp.sum(jnp.where(eye, sums, 0.0), axis=0, keepdims=True)
            stats[b, c : c + 1] = row.astype(jnp.bfloat16).astype(jnp.float32)

    per_block = HD // part

    for to in everyone:
        pltpu.make_async_remote_copy(
            src_ref=stats.at[to // per_block],
            dst_ref=stats_got.at[me],
            send_sem=stat_send,
            recv_sem=stat_recv,
            device_id={"frames": to},
        ).start()
    pltpu.make_async_copy(stats.at[me // per_block], stats_got.at[me], stat_recv).start()

    for c in range(1, clips):
        go(c, everyone)
        stay(c)

    def spatial(f):
        for copy in loads[f]:
            copy.wait()
        keys = spatial_in[1, f]
        values = spatial_in[2, f]
        for i in range(tokens // QB):
            rows = slice(i * QB, (i + 1) * QB)
            query = spatial_in[0, f, rows]
            grad = spatial_in[4, f, rows]
            rowdot = jnp.sum(
                grad.astype(jnp.float32) * spatial_in[3, f, rows].astype(jnp.float32),
                axis=-1,
                keepdims=True,
            )
            weights = softmax(dot(query, keys, 1, 1))
            dweights = dot(grad, values, 1, 1)
            dscores = (weights * (dweights - rowdot)).astype(jnp.bfloat16)
            dv = dot(weights.astype(jnp.bfloat16), grad, 0, 0)
            dk = dot(dscores, query, 0, 0)
            if i:
                dv = dv + dv_sum[...]
                dk = dk + dk_sum[...]
            if i < tokens // QB - 1:
                dv_sum[...] = dv
                dk_sum[...] = dk
            else:
                spatial_out[2, f] = dv.astype(jnp.bfloat16)
                spatial_out[1, f] = (dk * SCALE).astype(jnp.bfloat16)
            spatial_out[0, f, rows] = (dot(dscores, keys, 1, 0) * SCALE).astype(jnp.bfloat16)
        copies = []
        for i, ref in enumerate((dqs_hbm, dks_hbm, dvs_hbm)):
            copy = pltpu.make_async_copy(spatial_out.at[i, f], ref.at[f], out_sem.at[i, f])
            copy.start()
            copies.append(copy)
        return copies

    side = n * TG
    same_token = (
        lax.broadcasted_iota(jnp.int32, (side, side), 0) % TG
        == lax.broadcasted_iota(jnp.int32, (side, side), 1) % TG
    )

    def temporal(c):
        pltpu.make_async_copy(arrived.at[c], arrived.at[c], go_recv.at[c]).wait()
        if c == 0:
            pltpu.make_async_copy(stats_got, stats_got, stat_recv).wait()
        row_stats = (
            jnp.broadcast_to(stats_got[:, c : c + 1], (n, TG, HD))
            .reshape(side, HD)
            .astype(jnp.bfloat16)
        )
        lane = lax.broadcasted_iota(jnp.int32, (side, HD), 1)
        token = lax.broadcasted_iota(jnp.int32, (side, HD), 0) % TG
        first = lax.rem(me, per_block) * part
        for g in range(part // TG):
            rows = slice(g * TG, (g + 1) * TG)
            query = arrived[c, 0, :, rows].reshape(side, HD)
            keys = arrived[c, 1, :, rows].reshape(side, HD)
            values = arrived[c, 2, :, rows].reshape(side, HD)
            grad = arrived[c, 3, :, rows].reshape(side, HD)
            pick = jnp.where(lane == first + g * TG + token, -1.0, 0.0).astype(jnp.bfloat16)
            weights = softmax(jnp.where(same_token, dot(query, keys, 1, 1), -1e30))
            shifted = dot(grad, values, 1, 1) + dot(row_stats, pick, 1, 1)
            dscores = (weights * shifted).astype(jnp.bfloat16)
            dv = dot(weights.astype(jnp.bfloat16), grad, 0, 0)
            dq = dot(dscores, keys, 1, 0) * SCALE
            dk = dot(dscores, query, 0, 0) * SCALE
            for a, value in enumerate((dq, dk, dv)):
                leaving[c, a, :, rows] = value.astype(jnp.bfloat16).reshape(n, TG, HD)

        sends = [(a, to) for a in range(len(results)) for to in everyone]
        if c == clips - 1:
            sends = [(a, to) for to in everyone for a in range(len(results))]
        for a, to in sends:
            pltpu.make_async_remote_copy(
                src_ref=leaving.at[c, a, to],
                dst_ref=results[a].at[c, 0, mine],
                send_sem=back_send.at[a],
                recv_sem=back_recv.at[a],
                device_id={"frames": to},
            ).start()
        for a, ref in enumerate(results):
            pltpu.make_async_copy(
                leaving.at[c, a, me], ref.at[c, 0, mine], back_recv.at[a]
            ).start()

    copies = spatial(0)
    temporal(0)
    copies += spatial(1)
    temporal(1)

    for copy in copies:
        copy.wait()
    for c in range(clips):
        sent = arrived.at[c, :, pl.ds(0, n - 1)]
        pltpu.make_async_copy(sent, sent, go_send.at[c]).wait()
    sent = stats_got.at[pl.ds(0, n - 1)]
    pltpu.make_async_copy(sent, sent, stat_send).wait()
    for a, ref in enumerate(results):
        sent = leaving.at[:, a, pl.ds(0, n - 1)]
        pltpu.make_async_copy(sent, sent, back_send.at[a]).wait()
        pltpu.make_async_copy(ref, ref, back_recv.at[a]).wait()


def write_out(*refs):
    sources, targets, sem = refs[:6], refs[6:12], refs[12]
    copies = [pltpu.make_async_copy(sources[i], targets[i], sem.at[i]) for i in range(6)]
    for copy in copies:
        copy.start()
    for copy in copies:
        copy.wait()


def body(*args):
    n = lax.axis_size("frames")
    spatial, temporal = args[0], args[5]
    frames, tokens, _ = spatial.shape
    clips = temporal.shape[0]
    part = tokens // n
    hbm = pl.BlockSpec(memory_space=pltpu.HBM)
    anywhere = pl.BlockSpec(memory_space=pl.ANY)
    out_shape = [jax.ShapeDtypeStruct(spatial.shape, jnp.bfloat16)] * 3 + [
        jax.ShapeDtypeStruct(temporal.shape, jnp.bfloat16)
    ] * 3
    dma = pltpu.SemaphoreType.DMA
    gradients = pl.pallas_call(
        functools.partial(kernel, n),
        out_shape=out_shape,
        in_specs=[hbm] * 10,
        out_specs=[anywhere] * 6,
        scratch_shapes=[
            pltpu.VMEM((5, frames, tokens, HD), jnp.bfloat16),
            pltpu.VMEM((3, frames, tokens, HD), jnp.bfloat16),
            pltpu.VMEM((tokens, HD), jnp.float32),
            pltpu.VMEM((tokens, HD), jnp.float32),
            pltpu.VMEM((2, clips, tokens, HD), jnp.bfloat16),
            pltpu.VMEM((tokens // HD, clips, HD), jnp.float32),
            pltpu.VMEM((n, clips, HD), jnp.float32),
            pltpu.VMEM((clips, 4, n, part, HD), jnp.bfloat16),
            pltpu.VMEM((clips, 3, n, part, HD), jnp.bfloat16),
            dma((5, frames)),
            dma((3, frames)),
            dma((2,)),
            dma,
            dma,
            dma((clips,)),
            dma((clips,)),
            dma((3,)),
            dma((3,)),
            pltpu.SemaphoreType.REGULAR,
            pltpu.SemaphoreType.REGULAR,
        ],
        compiler_params=pltpu.CompilerParams(
            collective_id=0, has_side_effects=True, vmem_limit_bytes=VMEM_LIMIT
        ),
        cost_estimate=pl.CostEstimate(
            flops=5 * 2 * frames * tokens * tokens * HD,
            bytes_accessed=16 * frames * tokens * HD * 2,
            transcendentals=frames * tokens * tokens,
        ),
    )(*args)
    flat = [g.reshape(spatial.shape) for g in gradients]
    written = pl.pallas_call(
        write_out,
        out_shape=out_shape[:1] * 6,
        in_specs=[anywhere] * 6,
        out_specs=[hbm] * 6,
        scratch_shapes=[dma((6,))],
        compiler_params=pltpu.CompilerParams(vmem_limit_bytes=2 * 2**20),
    )(*flat)
    return tuple(g.reshape(o.shape) for o, g in zip(out_shape, written))


def solution(mesh):
    spatial = P("frames", None, "heads")
    temporal = P(None, "frames", None, "heads")
    return jax.shard_map(
        body,
        mesh=mesh,
        in_specs=(spatial,) * 5 + (temporal,) * 5,
        out_specs=(spatial,) * 3 + (temporal,) * 3,
        check_vma=False,
    )
```

```python
import functools
import math

import jax
import jax.numpy as jnp
from jax import lax
from jax.experimental import pallas as pl
from jax.experimental.pallas import tpu as pltpu
from jax.sharding import PartitionSpec as P

HD = 128
QB = 256
TG = 16
VMEM_LIMIT = 101 * 2**19
SCALE = HD**-0.5
NEAR = ((1, 0, 0), (0, 1, 0), (0, 3, 0), (1, 0, 1), (0, 1, 1), (0, 3, 1), (0, 0, 1))
MIDDLE = ((0, 2, 0), (1, 1, 0), (1, 3, 0), (0, 2, 1), (1, 1, 1), (1, 3, 1))
FAR = ((1, 2, 0), (1, 2, 1))
VMEM_LIMIT = 101 * 2**19
SCALE = HD**-0.5
STEPS = (
    (1, 2, 0), (1, 2, 1), (1, 1, 0), (1, 3, 1), (1, 3, 0), (1, 1, 1), (0, 2, 0), (1, 0, 1),
    (0, 2, 1), (1, 0, 0), (0, 1, 0), (0, 3, 1), (0, 3, 0), (0, 1, 1), (0, 0, 1),
)
EXP2_SCALE = SCALE * math.log2(math.e)


def dot(a, b, contract_a, contract_b):
    return lax.dot_general(
        a, b, (((contract_a,), (contract_b,)), ((), ())), preferred_element_type=jnp.float32
    )


def softmax(scores):
    top = jnp.max(scores, axis=-1, keepdims=True)
    powers = jnp.exp2((scores - top) * EXP2_SCALE)
    return powers * (1.0 / jnp.sum(powers, axis=-1, keepdims=True))


def kernel(
    n,
    qs_hbm, ks_hbm, vs_hbm, os_hbm, gs_hbm,
    qt_hbm, kt_hbm, vt_hbm, ot_hbm, gt_hbm,
    dqs_hbm, dks_hbm, dvs_hbm, dqt_hbm, dkt_hbm, dvt_hbm,
    spatial_in, spatial_out, dk_sum, dv_sum, stat_in, stats, stats_got, arrived, leaving,
    in_sem, out_sem, stat_in_sem, stat_send, stat_recv, go_send, go_recv, back_send, back_recv,
    near_sem, middle_sem,
):
    me = lax.axis_index("frames")
    clips, _, tokens, _ = qt_hbm.shape
    part = tokens // n
    mine = pl.ds(pl.multiple_of(me * part, part), part)
    payload = (qt_hbm, kt_hbm, vt_hbm, gt_hbm)
    results = (dqt_hbm, dkt_hbm, dvt_hbm)

    z, y, core = me // 8, lax.rem(me // 2, 4), lax.rem(me, 2)

    def at(step):
        dz, dy, dc = step
        return lax.rem(z + dz, 2) * 8 + lax.rem(y + dy, 4) * 2 + lax.rem(core + dc, 2)

    near, middle, far = ([at(step) for step in steps] for steps in (NEAR, MIDDLE, FAR))
    everyone = far + middle + near

    barrier = pltpu.get_barrier_semaphore()
    for to in near:
        pl.semaphore_signal(barrier, inc=1, device_id={"frames": to})

    def go(c, peers):
        for a, ref in enumerate(payload):
            for to in peers:
                rows = pl.ds(pl.multiple_of(to * part, part), part)
                pltpu.make_async_remote_copy(
                    src_ref=ref.at[c, 0, rows],
                    dst_ref=arrived.at[c, a, me],
                    send_sem=go_send.at[c],
                    recv_sem=go_recv.at[c],
                    device_id={"frames": to},
                ).start()

    def stay(c):
        for a, ref in enumerate(payload):
            pltpu.make_async_copy(
                ref.at[c, 0, mine], arrived.at[c, a, me], go_recv.at[c]
            ).start()

    pl.semaphore_wait(barrier, len(NEAR))
    go(0, near[:3])
    for step in NEAR[:3]:
        pl.semaphore_signal(near_sem, inc=1, device_id={"frames": at(step)})
    go(0, near[3:])

    stat_loads = []
    for i, ref in enumerate((gt_hbm, ot_hbm)):
        copy = pltpu.make_async_copy(ref.at[:, 0], stat_in.at[i], stat_in_sem.at[i])
        copy.start()
        stat_loads.append(copy)
    loads = []
    for f in range(clips):
        group = []
        for i, ref in enumerate((qs_hbm, ks_hbm, vs_hbm, os_hbm, gs_hbm)):
            copy = pltpu.make_async_copy(ref.at[f], spatial_in.at[i, f], in_sem.at[i, f])
            copy.start()
            group.append(copy)
        loads.append(group)

    stay(0)
    pl.semaphore_wait(near_sem, 3)
    pl.semaphore_signal(middle_sem, inc=1, device_id={"frames": at(NEAR[0])})
    go(0, middle)
    pl.semaphore_wait(middle_sem, 1)
    go(0, far)

    for copy in stat_loads:
        copy.wait()
    blocks = tokens // HD
    eye = lax.broadcasted_iota(jnp.int32, (HD, HD), 0) == lax.broadcasted_iota(
        jnp.int32, (HD, HD), 1
    )
    for c in range(clips):
        for b in range(blocks):
            rows = slice(b * HD, (b + 1) * HD)
            products = stat_in[0, c, rows].astype(jnp.float32) * stat_in[1, c, rows].astype(
                jnp.float32
            )
            sums = jnp.sum(products, axis=-1, keepdims=True)
            row = jnp.sum(jnp.where(eye, sums, 0.0), axis=0, keepdims=True)
            stats[b, c : c + 1] = row.astype(jnp.bfloat16).astype(jnp.float32)

    per_block = HD // part

    for to in everyone:
        pltpu.make_async_remote_copy(
            src_ref=stats.at[to // per_block],
            dst_ref=stats_got.at[me],
            send_sem=stat_send,
            recv_sem=stat_recv,
            device_id={"frames": to},
        ).start()
    pltpu.make_async_copy(stats.at[me // per_block], stats_got.at[me], stat_recv).start()

    for c in range(1, clips):
        go(c, everyone)
        stay(c)

    def spatial(f):
        for copy in loads[f]:
            copy.wait()
        dv_sum[...] = jnp.zeros_like(dv_sum)
        dk_sum[...] = jnp.zeros_like(dk_sum)

        def step(i, carry):
            rows = pl.ds(pl.multiple_of(i * QB, QB), QB)
            keys = spatial_in[1, f]
            query = spatial_in[0, f, rows]
            grad = spatial_in[4, f, rows]
            rowdot = jnp.sum(
                grad.astype(jnp.float32) * spatial_in[3, f, rows].astype(jnp.float32),
                axis=-1,
                keepdims=True,
            )
            weights = softmax(dot(query, keys, 1, 1))
            dweights = dot(grad, spatial_in[2, f], 1, 1)
            dscores = (weights * (dweights - rowdot)).astype(jnp.bfloat16)
            dv_sum[...] += dot(weights.astype(jnp.bfloat16), grad, 0, 0)
            dk_sum[...] += dot(dscores, query, 0, 0)
            spatial_out[0, f, rows] = (dot(dscores, keys, 1, 0) * SCALE).astype(jnp.bfloat16)
            return carry

        lax.fori_loop(0, tokens // QB, step, 0)
        spatial_out[2, f] = dv_sum[...].astype(jnp.bfloat16)
        spatial_out[1, f] = (dk_sum[...] * SCALE).astype(jnp.bfloat16)
        copies = []
        for i, ref in enumerate((dqs_hbm, dks_hbm, dvs_hbm)):
            copy = pltpu.make_async_copy(spatial_out.at[i, f], ref.at[f], out_sem.at[i, f])
            copy.start()
            copies.append(copy)
        return copies

    side = n * TG
    same_token = (
        lax.broadcasted_iota(jnp.int32, (side, side), 0) % TG
        == lax.broadcasted_iota(jnp.int32, (side, side), 1) % TG
    )

    def temporal(c):
        pltpu.make_async_copy(arrived.at[c], arrived.at[c], go_recv.at[c]).wait()
        if c == 0:
            pltpu.make_async_copy(stats_got, stats_got, stat_recv).wait()
        row_stats = (
            jnp.broadcast_to(stats_got[:, c : c + 1], (n, TG, HD))
            .reshape(side, HD)
            .astype(jnp.bfloat16)
        )
        lane = lax.broadcasted_iota(jnp.int32, (side, HD), 1)
        token = lax.broadcasted_iota(jnp.int32, (side, HD), 0) % TG
        first = lax.rem(me, per_block) * part
        def group(g, carry):
            rows = pl.ds(pl.multiple_of(g * TG, TG), TG)
            query = arrived[c, 0, :, rows].reshape(side, HD)
            keys = arrived[c, 1, :, rows].reshape(side, HD)
            values = arrived[c, 2, :, rows].reshape(side, HD)
            grad = arrived[c, 3, :, rows].reshape(side, HD)
            pick = jnp.where(lane == first + g * TG + token, -1.0, 0.0).astype(jnp.bfloat16)
            weights = softmax(jnp.where(same_token, dot(query, keys, 1, 1), -1e30))
            shifted = dot(grad, values, 1, 1) + dot(row_stats, pick, 1, 1)
            dscores = (weights * shifted).astype(jnp.bfloat16)
            dv = dot(weights.astype(jnp.bfloat16), grad, 0, 0)
            dq = dot(dscores, keys, 1, 0) * SCALE
            dk = dot(dscores, query, 0, 0) * SCALE
            for a, value in enumerate((dq, dk, dv)):
                leaving[c, a, :, rows] = value.astype(jnp.bfloat16).reshape(n, TG, HD)
            return carry

        lax.fori_loop(0, part // TG, group, 0)

        sends = [(a, to) for a in range(len(results)) for to in everyone]
        if c == clips - 1:
            sends = [(a, to) for to in everyone for a in range(len(results))]
        for a, to in sends:
            pltpu.make_async_remote_copy(
                src_ref=leaving.at[c, a, to],
                dst_ref=results[a].at[c, 0, mine],
                send_sem=back_send.at[a],
                recv_sem=back_recv.at[a],
                device_id={"frames": to},
            ).start()
        for a, ref in enumerate(results):
            pltpu.make_async_copy(
                leaving.at[c, a, me], ref.at[c, 0, mine], back_recv.at[a]
            ).start()

    copies = spatial(0)
    temporal(0)
    copies += spatial(1)
    temporal(1)

    for copy in copies:
        copy.wait()
    for c in range(clips):
        sent = arrived.at[c, :, pl.ds(0, n - 1)]
        pltpu.make_async_copy(sent, sent, go_send.at[c]).wait()
    sent = stats_got.at[pl.ds(0, n - 1)]
    pltpu.make_async_copy(sent, sent, stat_send).wait()
    for a, ref in enumerate(results):
        sent = leaving.at[:, a, pl.ds(0, n - 1)]
        pltpu.make_async_copy(sent, sent, back_send.at[a]).wait()
        pltpu.make_async_copy(ref, ref, back_recv.at[a]).wait()


def write_out(*refs):
    sources, targets, sem = refs[:6], refs[6:12], refs[12]
    copies = [pltpu.make_async_copy(sources[i], targets[i], sem.at[i]) for i in range(6)]
    for copy in copies:
        copy.start()
    for copy in copies:
        copy.wait()


def body(*args):
    n = lax.axis_size("frames")
    spatial, temporal = args[0], args[5]
    frames, tokens, _ = spatial.shape
    clips = temporal.shape[0]
    part = tokens // n
    hbm = pl.BlockSpec(memory_space=pltpu.HBM)
    anywhere = pl.BlockSpec(memory_space=pl.ANY)
    out_shape = [jax.ShapeDtypeStruct(spatial.shape, jnp.bfloat16)] * 3 + [
        jax.ShapeDtypeStruct(temporal.shape, jnp.bfloat16)
    ] * 3
    dma = pltpu.SemaphoreType.DMA
    gradients = pl.pallas_call(
        functools.partial(kernel, n),
        out_shape=out_shape,
        in_specs=[hbm] * 10,
        out_specs=[anywhere] * 6,
        scratch_shapes=[
            pltpu.VMEM((5, frames, tokens, HD), jnp.bfloat16),
            pltpu.VMEM((3, frames, tokens, HD), jnp.bfloat16),
            pltpu.VMEM((tokens, HD), jnp.float32),
            pltpu.VMEM((tokens, HD), jnp.float32),
            pltpu.VMEM((2, clips, tokens, HD), jnp.bfloat16),
            pltpu.VMEM((tokens // HD, clips, HD), jnp.float32),
            pltpu.VMEM((n, clips, HD), jnp.float32),
            pltpu.VMEM((clips, 4, n, part, HD), jnp.bfloat16),
            pltpu.VMEM((clips, 3, n, part, HD), jnp.bfloat16),
            dma((5, frames)),
            dma((3, frames)),
            dma((2,)),
            dma,
            dma,
            dma((clips,)),
            dma((clips,)),
            dma((3,)),
            dma((3,)),
            pltpu.SemaphoreType.REGULAR,
            pltpu.SemaphoreType.REGULAR,
        ],
        compiler_params=pltpu.CompilerParams(
            collective_id=0, has_side_effects=True, vmem_limit_bytes=VMEM_LIMIT
        ),
        cost_estimate=pl.CostEstimate(
            flops=5 * 2 * frames * tokens * tokens * HD,
            bytes_accessed=16 * frames * tokens * HD * 2,
            transcendentals=frames * tokens * tokens,
        ),
    )(*args)
    flat = [g.reshape(spatial.shape) for g in gradients]
    written = pl.pallas_call(
        write_out,
        out_shape=out_shape[:1] * 6,
        in_specs=[anywhere] * 6,
        out_specs=[hbm] * 6,
        scratch_shapes=[dma((6,))],
        compiler_params=pltpu.CompilerParams(vmem_limit_bytes=2 * 2**20),
    )(*flat)
    return tuple(g.reshape(o.shape) for o, g in zip(out_shape, written))


def solution(mesh):
    spatial = P("frames", None, "heads")
    temporal = P(None, "frames", None, "heads")
    return jax.shard_map(
        body,
        mesh=mesh,
        in_specs=(spatial,) * 5 + (temporal,) * 5,
        out_specs=(spatial,) * 3 + (temporal,) * 3,
        check_vma=False,
    )
```

```python
import functools
import math

import jax
import jax.numpy as jnp
from jax import lax
from jax.experimental import pallas as pl
from jax.experimental.pallas import tpu as pltpu
from jax.sharding import PartitionSpec as P

HD = 128
QB = 256
TG = 16
VMEM_LIMIT = 101 * 2**19
SCALE = HD**-0.5
NEAR = ((1, 0, 0), (0, 1, 0), (0, 3, 0), (1, 0, 1), (0, 1, 1), (0, 3, 1), (0, 0, 1))
MIDDLE = ((0, 2, 0), (1, 1, 0), (1, 3, 0), (0, 2, 1), (1, 1, 1), (1, 3, 1))
FAR = ((1, 2, 0), (1, 2, 1))
VMEM_LIMIT = 101 * 2**19
SCALE = HD**-0.5
STEPS = (
    (1, 2, 0), (1, 2, 1), (1, 1, 0), (1, 3, 1), (1, 3, 0), (1, 1, 1), (0, 2, 0), (1, 0, 1),
    (0, 2, 1), (1, 0, 0), (0, 1, 0), (0, 3, 1), (0, 3, 0), (0, 1, 1), (0, 0, 1),
)
EXP2_SCALE = SCALE * math.log2(math.e)


def dot(a, b, contract_a, contract_b):
    return lax.dot_general(
        a, b, (((contract_a,), (contract_b,)), ((), ())), preferred_element_type=jnp.float32
    )


def softmax(scores):
    top = jnp.max(scores, axis=-1, keepdims=True)
    powers = jnp.exp2((scores - top) * EXP2_SCALE)
    return powers * (1.0 / jnp.sum(powers, axis=-1, keepdims=True))


def kernel(
    n,
    qs_hbm, ks_hbm, vs_hbm, os_hbm, gs_hbm,
    qt_hbm, kt_hbm, vt_hbm, ot_hbm, gt_hbm,
    dqs_hbm, dks_hbm, dvs_hbm, dqt_hbm, dkt_hbm, dvt_hbm,
    spatial_in, spatial_out, dk_sum, dv_sum, stat_in, stats, stats_got, arrived, leaving,
    in_sem, out_sem, stat_in_sem, stat_send, stat_recv, go_send, go_recv, back_send, back_recv,
    near_sem, middle_sem,
):
    me = lax.axis_index("frames")
    clips, _, tokens, _ = qt_hbm.shape
    part = tokens // n
    mine = pl.ds(pl.multiple_of(me * part, part), part)
    payload = (qt_hbm, kt_hbm, vt_hbm, gt_hbm)
    results = (dqt_hbm, dkt_hbm, dvt_hbm)

    z, y, core = me // 8, lax.rem(me // 2, 4), lax.rem(me, 2)

    def at(step):
        dz, dy, dc = step
        return lax.rem(z + dz, 2) * 8 + lax.rem(y + dy, 4) * 2 + lax.rem(core + dc, 2)

    near, middle, far = ([at(step) for step in steps] for steps in (NEAR, MIDDLE, FAR))
    everyone = far + middle + near

    barrier = pltpu.get_barrier_semaphore()
    for to in near:
        pl.semaphore_signal(barrier, inc=1, device_id={"frames": to})

    def go(c, peers):
        for a, ref in enumerate(payload):
            for to in peers:
                rows = pl.ds(pl.multiple_of(to * part, part), part)
                pltpu.make_async_remote_copy(
                    src_ref=ref.at[c, 0, rows],
                    dst_ref=arrived.at[c, a, me],
                    send_sem=go_send.at[c],
                    recv_sem=go_recv.at[c],
                    device_id={"frames": to},
                ).start()

    def stay(c):
        for a, ref in enumerate(payload):
            pltpu.make_async_copy(
                ref.at[c, 0, mine], arrived.at[c, a, me], go_recv.at[c]
            ).start()

    pl.semaphore_wait(barrier, len(NEAR))
    go(0, near[:3])
    for step in NEAR[:3]:
        pl.semaphore_signal(near_sem, inc=1, device_id={"frames": at(step)})
    go(0, near[3:])

    stat_loads = []
    for i, ref in enumerate((gt_hbm, ot_hbm)):
        copy = pltpu.make_async_copy(ref.at[:, 0], stat_in.at[i], stat_in_sem.at[i])
        copy.start()
        stat_loads.append(copy)
    for f in range(clips):
        for i, ref in enumerate((qs_hbm, ks_hbm, vs_hbm, os_hbm, gs_hbm)):
            pltpu.make_async_copy(ref.at[f], spatial_in.at[i, f], in_sem.at[i, f]).start()
    stay(0)
    pl.semaphore_wait(near_sem, 3)
    pl.semaphore_signal(middle_sem, inc=1, device_id={"frames": at(NEAR[0])})
    go(0, middle)
    pl.semaphore_wait(middle_sem, 1)
    go(0, far)

    for copy in stat_loads:
        copy.wait()
    blocks = tokens // HD
    eye = lax.broadcasted_iota(jnp.int32, (HD, HD), 0) == lax.broadcasted_iota(
        jnp.int32, (HD, HD), 1
    )
    for c in range(clips):
        for b in range(blocks):
            rows = slice(b * HD, (b + 1) * HD)
            products = stat_in[0, c, rows].astype(jnp.float32) * stat_in[1, c, rows].astype(
                jnp.float32
            )
            sums = jnp.sum(products, axis=-1, keepdims=True)
            row = jnp.sum(jnp.where(eye, sums, 0.0), axis=0, keepdims=True)
            stats[b, c : c + 1] = row.astype(jnp.bfloat16).astype(jnp.float32)

    per_block = HD // part

    for to in everyone:
        pltpu.make_async_remote_copy(
            src_ref=stats.at[to // per_block],
            dst_ref=stats_got.at[me],
            send_sem=stat_send,
            recv_sem=stat_recv,
            device_id={"frames": to},
        ).start()
    pltpu.make_async_copy(stats.at[me // per_block], stats_got.at[me], stat_recv).start()

    for c in range(1, clips):
        go(c, everyone)
        stay(c)

    def spatial(f):
        for i in range(5):
            held = spatial_in.at[i, f]
            pltpu.make_async_copy(held, held, in_sem.at[i, f]).wait()
        dv_sum[...] = jnp.zeros_like(dv_sum)
        dk_sum[...] = jnp.zeros_like(dk_sum)

        def step(i, carry):
            rows = pl.ds(pl.multiple_of(i * QB, QB), QB)
            keys = spatial_in[1, f]
            query = spatial_in[0, f, rows]
            grad = spatial_in[4, f, rows]
            rowdot = jnp.sum(
                grad.astype(jnp.float32) * spatial_in[3, f, rows].astype(jnp.float32),
                axis=-1,
                keepdims=True,
            )
            weights = softmax(dot(query, keys, 1, 1))
            dweights = dot(grad, spatial_in[2, f], 1, 1)
            dscores = (weights * (dweights - rowdot)).astype(jnp.bfloat16)
            dv_sum[...] += dot(weights.astype(jnp.bfloat16), grad, 0, 0)
            dk_sum[...] += dot(dscores, query, 0, 0)
            spatial_out[0, f, rows] = (dot(dscores, keys, 1, 0) * SCALE).astype(jnp.bfloat16)
            return carry

        lax.fori_loop(0, tokens // QB, step, 0)
        spatial_out[2, f] = dv_sum[...].astype(jnp.bfloat16)
        spatial_out[1, f] = (dk_sum[...] * SCALE).astype(jnp.bfloat16)
        for i, ref in enumerate((dqs_hbm, dks_hbm, dvs_hbm)):
            pltpu.make_async_copy(spatial_out.at[i, f], ref.at[f], out_sem.at[i]).start()

    side = n * TG
    same_token = (
        lax.broadcasted_iota(jnp.int32, (side, side), 0) % TG
        == lax.broadcasted_iota(jnp.int32, (side, side), 1) % TG
    )

    def temporal(c):
        pltpu.make_async_copy(arrived.at[c], arrived.at[c], go_recv.at[c]).wait()

        @pl.when(c == 0)
        def _():
            pltpu.make_async_copy(stats_got, stats_got, stat_recv).wait()

        row_stats = (
            jnp.broadcast_to(stats_got[:, pl.ds(c, 1)], (n, TG, HD))
            .reshape(side, HD)
            .astype(jnp.bfloat16)
        )
        lane = lax.broadcasted_iota(jnp.int32, (side, HD), 1)
        token = lax.broadcasted_iota(jnp.int32, (side, HD), 0) % TG
        first = lax.rem(me, per_block) * part
        def group(g, carry):
            rows = pl.ds(pl.multiple_of(g * TG, TG), TG)
            query = arrived[c, 0, :, rows].reshape(side, HD)
            keys = arrived[c, 1, :, rows].reshape(side, HD)
            values = arrived[c, 2, :, rows].reshape(side, HD)
            grad = arrived[c, 3, :, rows].reshape(side, HD)
            pick = jnp.where(lane == first + g * TG + token, -1.0, 0.0).astype(jnp.bfloat16)
            weights = softmax(jnp.where(same_token, dot(query, keys, 1, 1), -1e30))
            shifted = dot(grad, values, 1, 1) + dot(row_stats, pick, 1, 1)
            dscores = (weights * shifted).astype(jnp.bfloat16)
            dv = dot(weights.astype(jnp.bfloat16), grad, 0, 0)
            dq = dot(dscores, keys, 1, 0) * SCALE
            dk = dot(dscores, query, 0, 0) * SCALE
            for a, value in enumerate((dq, dk, dv)):
                leaving[c, a, :, rows] = value.astype(jnp.bfloat16).reshape(n, TG, HD)
            return carry

        lax.fori_loop(0, part // TG, group, 0)

        sends = [(a, to) for to in everyone for a in range(len(results))]
        for a, to in sends:
            pltpu.make_async_remote_copy(
                src_ref=leaving.at[c, a, to],
                dst_ref=results[a].at[c, 0, mine],
                send_sem=back_send.at[a],
                recv_sem=back_recv.at[a],
                device_id={"frames": to},
            ).start()
        for a, ref in enumerate(results):
            pltpu.make_async_copy(
                leaving.at[c, a, me], ref.at[c, 0, mine], back_recv.at[a]
            ).start()

    def both(c, carry):
        spatial(c)
        temporal(c)
        return carry

    lax.fori_loop(0, clips, both, 0)

    for i, ref in enumerate((dqs_hbm, dks_hbm, dvs_hbm)):
        pltpu.make_async_copy(spatial_out.at[i], ref, out_sem.at[i]).wait()
    for c in range(clips):
        sent = arrived.at[c, :, pl.ds(0, n - 1)]
        pltpu.make_async_copy(sent, sent, go_send.at[c]).wait()
    sent = stats_got.at[pl.ds(0, n - 1)]
    pltpu.make_async_copy(sent, sent, stat_send).wait()
    for a, ref in enumerate(results):
        sent = leaving.at[:, a, pl.ds(0, n - 1)]
        pltpu.make_async_copy(sent, sent, back_send.at[a]).wait()
        pltpu.make_async_copy(ref, ref, back_recv.at[a]).wait()


def write_out(*refs):
    sources, targets, sem = refs[:6], refs[6:12], refs[12]
    copies = [pltpu.make_async_copy(sources[i], targets[i], sem.at[i]) for i in range(6)]
    for copy in copies:
        copy.start()
    for copy in copies:
        copy.wait()


def body(*args):
    n = lax.axis_size("frames")
    spatial, temporal = args[0], args[5]
    frames, tokens, _ = spatial.shape
    clips = temporal.shape[0]
    part = tokens // n
    hbm = pl.BlockSpec(memory_space=pltpu.HBM)
    anywhere = pl.BlockSpec(memory_space=pl.ANY)
    out_shape = [jax.ShapeDtypeStruct(spatial.shape, jnp.bfloat16)] * 3 + [
        jax.ShapeDtypeStruct(temporal.shape, jnp.bfloat16)
    ] * 3
    dma = pltpu.SemaphoreType.DMA
    gradients = pl.pallas_call(
        functools.partial(kernel, n),
        out_shape=out_shape,
        in_specs=[hbm] * 10,
        out_specs=[anywhere] * 6,
        scratch_shapes=[
            pltpu.VMEM((5, frames, tokens, HD), jnp.bfloat16),
            pltpu.VMEM((3, frames, tokens, HD), jnp.bfloat16),
            pltpu.VMEM((tokens, HD), jnp.float32),
            pltpu.VMEM((tokens, HD), jnp.float32),
            pltpu.VMEM((2, clips, tokens, HD), jnp.bfloat16),
            pltpu.VMEM((tokens // HD, clips, HD), jnp.float32),
            pltpu.VMEM((n, clips, HD), jnp.float32),
            pltpu.VMEM((clips, 4, n, part, HD), jnp.bfloat16),
            pltpu.VMEM((clips, 3, n, part, HD), jnp.bfloat16),
            dma((5, frames)),
            dma((3,)),
            dma((2,)),
            dma,
            dma,
            dma((clips,)),
            dma((clips,)),
            dma((3,)),
            dma((3,)),
            pltpu.SemaphoreType.REGULAR,
            pltpu.SemaphoreType.REGULAR,
        ],
        compiler_params=pltpu.CompilerParams(
            collective_id=0, has_side_effects=True, vmem_limit_bytes=VMEM_LIMIT
        ),
        cost_estimate=pl.CostEstimate(
            flops=5 * 2 * frames * tokens * tokens * HD,
            bytes_accessed=16 * frames * tokens * HD * 2,
            transcendentals=frames * tokens * tokens,
        ),
    )(*args)
    flat = [g.reshape(spatial.shape) for g in gradients]
    written = pl.pallas_call(
        write_out,
        out_shape=out_shape[:1] * 6,
        in_specs=[anywhere] * 6,
        out_specs=[hbm] * 6,
        scratch_shapes=[dma((6,))],
        compiler_params=pltpu.CompilerParams(vmem_limit_bytes=2 * 2**20),
    )(*flat)
    return tuple(g.reshape(o.shape) for o, g in zip(out_shape, written))


def solution(mesh):
    spatial = P("frames", None, "heads")
    temporal = P(None, "frames", None, "heads")
    return jax.shard_map(
        body,
        mesh=mesh,
        in_specs=(spatial,) * 5 + (temporal,) * 5,
        out_specs=(spatial,) * 3 + (temporal,) * 3,
        check_vma=False,
    )
```
